32 devices in a mesh: row: 4 (over y, x), col: 8 (over z, core).
Axes of the slice: x: 2, y: 2, z: 4, core: 2. Of those that a mesh axis runs over, the one named last changes fastest.
Arguments:
- amplitude: float32 [800, 20480], P('row', 'col'), may hold values from -6 to 6
- ladder_coupling: float32 [20480, 20480], P('row', 'col'), may hold values from -0.0390625 to 0.0390625
- crossed_coupling: float32 [4, 1280, 1280], P('row'), may hold values from -0.15625 to 0.15625
- channel_slot: int32 [4], replicated, may hold values from 0 to 3, each once
- channel_of: int32 [8, 512, 1], P('col', 'row'), may hold values from 0 to 3; in each aligned block of 128 rows (0 to 127, 128 to 255, ..., all dimensions but the last counted through in order) at most 40 rows name the same one
- source_row: int32 [8, 512], P('col', 'row'), may hold values from 0 to 1599
- target_row: int32 [8, 512], P('col', 'row'), may hold values from 0 to 3199
- recoupling: float32 [8, 512], P('col', 'row'), may hold values from -1 to 1
- driving: float32 [800, 20480], P('col', 'row'), may hold values from -6 to 6
- denominator: float32 [800, 20480], P('col', 'row'), may hold values from 1 to 10
Outputs:
- updated: float32 [800, 20480], P('col', 'row')
The draws below stay inside these ranges and needn't reach their ends.
Inputs may be any that keep to these rules, and one draw needn't show every extreme that they name: Among the 128 segments of one device (aligned blocks of channel_of's rows), no channel is named more than 40 times; some channel is named exactly 40 times in some device's segments. `channel_slot`: each slot once.
All inputs are finite; a program needn't handle non-finite values.
Results may differ from the reference program's by a relative error of at most 0.0003.
Values sent between devices are 32-bit elements; how exact they have to be, the bound alone decides.
No kernel may reach another device: no remote copies, remote signals or barrier semaphores. Data moves between devices by JAX's collectives and lax.ppermute only.
A program may use at most 192 MiB of HBM per device.

```python
import math
import jax
import jax.numpy as jnp
import numpy as np
from jax import lax

H = 800
P_SIZE = 20480
W = 1280
ITEMS = 128
NCH = 4
CAP = 40
ITEMS_ALL = 512
SEG_IN = 2
SEG_OUT = 4
N_ROW = 4
N_COL = 8


def set_ends(values, own_key, least, high):
    longest = values.shape.index(max(values.shape))
    spots = []
    for shift in (0, 1):
        where = [jax.random.randint(jax.random.fold_in(own_key, axis), (), 0, length) for axis, length in enumerate(values.shape)]
        where[longest] = (where[longest] + shift) % values.shape[longest]
        spots.append(tuple(where))
    return values.at[spots[0]].set(least).at[spots[1]].set(high)


def block_levels(rng, extent, shards, least, top_value):
    gain = 1.0
    for dim, blocks in shards:
        heights = jax.random.uniform(jax.random.fold_in(jax.random.fold_in(rng, 6), dim), (blocks,), jnp.float32, least / len(shards), top_value / len(shards))
        gain = gain * jnp.repeat(jnp.exp(heights), extent[dim] // blocks).reshape((-1,) + (1,) * (len(extent) - 1 - dim))
    return gain


def shared_out(stream_key, own, number, rows, number_of, top, most, skew):
    sequence = jax.random.permutation(stream_key, number_of)
    crowded, common = load_shares(number_of, rows * top, most, skew, True), load_shares(number_of, rows * top, most, skew, False)
    places = jnp.arange(number_of)

    def named(tallies, turn):
        used = int((tallies > 0).sum())
        fixed = max(1, used // 4)
        shifted = fixed + (places - fixed + turn * (used - fixed)) % max(1, number_of - fixed)
        return jnp.zeros((number_of,), jnp.int32).at[sequence[jnp.where(places < fixed, places, shifted)]].set(jnp.asarray(tallies, jnp.int32))

    tallies = jnp.where(number % 4 == 0, named(crowded, number // 4), named(common, number - number // 4 - 1))
    mixed = jax.random.permutation(jax.random.fold_in(own, 3), number_of)
    donor, sink = mixed[0:number_of // 2 * 2:2], mixed[1:number_of // 2 * 2:2]
    slack = jnp.minimum(tallies[donor] - 1, most - tallies[sink]) // 2
    slack = jnp.where((donor == sequence[0]) | (sink == sequence[0]) | (tallies[sink] == 0), 0, jnp.maximum(slack, 0))
    shifted = jax.random.randint(jax.random.fold_in(own, 4), (number_of // 2,), 0, 1 << 20) % (slack + 1)
    tallies = tallies.at[donor].add(-shifted).at[sink].add(shifted)
    members = jnp.searchsorted(jnp.cumsum(tallies), jnp.arange(rows * top), side="right").astype(jnp.int32)
    grid = members.reshape(top, rows).T
    grid = grid[jax.random.permutation(jax.random.fold_in(own, 1), rows)]
    turn = jax.random.randint(jax.random.fold_in(own, 2), (rows, 1), 0, top)
    return jnp.take_along_axis(grid, (jnp.arange(top)[None, :] + turn) % top, axis=1)


def load_shares(count, total, most, lean, full):
    loads = [(1 << 20) // math.isqrt(rank ** lean) + 1 for rank in range(1, count + 1)]
    largest = most if full else min(most, max(-(-total // count), total * loads[0] // sum(loads)))
    least = 1 if total - largest >= count - 1 else 0
    holding, spare = [largest] + [least] * (count - 1), total - largest - least * (count - 1)
    while spare > 0:
        movable = [i for i in range(1, count) if holding[i] < largest] or [i for i in range(1, count) if holding[i] < most]
        mass, left = sum([loads[i] for i in movable]), spare
        for i in movable:
            more = min(most - holding[i], max(1, left * loads[i] // mass), spare)
            holding[i] = holding[i] + more
            spare = spare - more
    return np.array(holding)


def scatter_about(rng, dims, width, reach, split=(), kind=jnp.bfloat16):
    drawn = jax.random.normal(rng, dims, jnp.float32) * width
    if len(split) > 0:
        drawn = block_levels(rng, dims, split, -0.22, 0.18) * drawn
    return jnp.clip(drawn, min=-reach, max=reach).astype(kind)


def setup_inputs(seed: int = 0) -> dict:
    key_of = jax.random.split(jax.random.key(seed), 11)
    amplitude = scatter_about(key_of[0], (H, P_SIZE), 1.0, 6.0, ((0, 4), (1, 8)), jnp.float32)
    ladder_coupling = scatter_about(key_of[1], (P_SIZE, P_SIZE), P_SIZE ** -0.5, 0.0390625, ((0, 4), (1, 8)), jnp.float32)
    crossed_coupling = scatter_about(key_of[2], (NCH, W, W), W ** -0.5, 0.15625, ((0, 4),), jnp.float32)
    channel_slot = jax.random.permutation(key_of[3], NCH).astype(jnp.int32)
    channel_of_keys = jax.random.split(jax.random.fold_in(key_of[4], 1), N_COL * ITEMS_ALL // ITEMS)
    channel_of_turns = jax.random.permutation(jax.random.fold_in(key_of[4], 3), N_COL * ITEMS_ALL // ITEMS)
    channel_of = jax.vmap(lambda own, number: shared_out(jax.random.fold_in(key_of[4], 2), own, number, ITEMS, NCH, 1, CAP, 2))(channel_of_keys, channel_of_turns).reshape((N_COL, ITEMS_ALL, 1))
    source_row = set_ends(jax.random.randint(key_of[5], (N_COL, ITEMS_ALL), 0, H * SEG_IN), jax.random.fold_in(key_of[5], 1), 0, (H * SEG_IN) - 1).astype(jnp.int32)
    target_row = set_ends(jax.random.randint(key_of[6], (N_COL, ITEMS_ALL), 0, H * SEG_OUT), jax.random.fold_in(key_of[6], 1), 0, (H * SEG_OUT) - 1).astype(jnp.int32)
    recoupling = jnp.clip(jax.random.uniform(key_of[7], (N_COL, ITEMS_ALL), jnp.float32, -1.0, 1.0) * block_levels(key_of[7], (N_COL, ITEMS_ALL), ((0, 8), (1, 4)), -0.4, 0.0), -1.0, 1.0)
    driving = scatter_about(key_of[8], (H, P_SIZE), 1.0, 6.0, ((0, 8), (1, 4)), jnp.float32)
    denominator = jnp.clip(jnp.exp(math.log(10.0) - 2.3025851 * jax.random.uniform(key_of[9], (H, P_SIZE), jnp.float32) ** block_levels(key_of[9], (H, P_SIZE), ((0, 8), (1, 4)), -0.2, 0.2)), 1.0, 10.0)
    return {"amplitude": amplitude, "ladder_coupling": ladder_coupling, "crossed_coupling": crossed_coupling, "channel_slot": channel_slot, "channel_of": channel_of, "source_row": source_row, "target_row": target_row, "recoupling": recoupling, "driving": driving, "denominator": denominator}


def reference(amplitude, ladder_coupling, crossed_coupling, channel_slot, channel_of, source_row, target_row, recoupling, driving, denominator):
    highest = lax.Precision.HIGHEST
    ladder = lax.dot_general(amplitude, ladder_coupling, (((1,), (1,)), ((), ())), precision=highest, preferred_element_type=jnp.float32)
    blocks = amplitude.reshape(H, N_COL, SEG_IN, W).transpose(1, 0, 2, 3).reshape(N_COL, H * SEG_IN, W)
    picked = jax.vmap(lambda table_rows, chosen: table_rows[chosen])(blocks, source_row)
    picked = picked * recoupling[:, :, None]
    owners = channel_slot[channel_of[:, :, 0]]

    def add_channel(accumulated, slot_id):
        matrix = lax.dynamic_index_in_dim(crossed_coupling, slot_id, 0, keepdims=False)
        product = jnp.einsum("cnw,wv->cnv", picked, matrix, precision=highest, preferred_element_type=jnp.float32)
        return accumulated + jnp.where((owners == slot_id)[:, :, None], product, jnp.float32(0.0)), None

    crossed, _ = lax.scan(add_channel, jnp.zeros(picked.shape, jnp.float32), jnp.arange(NCH, dtype=jnp.int32))
    hole_index = target_row // SEG_OUT
    segment_index = target_row % SEG_OUT
    block_index = jnp.broadcast_to((jnp.arange(ITEMS_ALL, dtype=jnp.int32) // ITEMS)[None, :], target_row.shape)
    particle_hole = jnp.zeros((H, N_ROW, SEG_OUT, W), jnp.float32).at[hole_index, block_index, segment_index].add(crossed)
    particle_hole = particle_hole.reshape(H, P_SIZE)
    return (driving + ladder + particle_hole) / denominator
```

```python
import functools

import jax
import jax.numpy as jnp
from jax import lax
from jax.experimental import pallas as pl
from jax.experimental.pallas import tpu as pltpu
from jax.sharding import PartitionSpec as P

CAP = 40
F32 = jnp.float32
BF16 = jnp.bfloat16
VMEM_LIMIT = 56 * 1024 * 1024


def chunk_sizes(total):
    sizes, left = [8], total - 8
    while left > 0:
        sizes.append(min(32, left))
        left -= sizes[-1]
    return sizes


def halves(x):
    high = x.astype(BF16)
    return high, (x - high.astype(F32)).astype(BF16)


def dot(x, y, contract):
    return lax.dot_general(x, y, ((contract[0], contract[1]), ((), ())), preferred_element_type=F32)


def ladder_kernel(n_pieces, half_ref, *refs):
    pieces, coupling_ref, out_ref, high_ref, low_ref = refs[:n_pieces], *refs[n_pieces:]

    @pl.when(pl.program_id(0) == 0)
    def _():
        high, low = halves(jnp.concatenate([piece[...] for piece in pieces], axis=0))
        high_ref[...] = high
        low_ref[...] = low

    coupling_high, coupling_low = halves(coupling_ref[...])
    nt = ((1,), (1,))
    value = dot(high_ref[...], coupling_high, nt)
    value += dot(low_ref[...], coupling_high, nt) + dot(high_ref[...], coupling_low, nt)
    out_ref[...] = value.reshape(out_ref.shape)


def ladder(half, pieces, coupling, width):
    n_pieces = len(pieces)
    rows, inner = pieces[0].shape
    part = width // 2
    segments = coupling.shape[0] // width
    total = n_pieces * rows
    return pl.pallas_call(
        functools.partial(ladder_kernel, n_pieces),
        grid_spec=pltpu.PrefetchScalarGridSpec(
            num_scalar_prefetch=1,
            grid=(segments,),
            in_specs=[pl.BlockSpec((rows, inner), lambda i, half: (0, 0))] * n_pieces
            + [pl.BlockSpec((part, inner), lambda i, half: (2 * i + half[0], 0))],
            out_specs=pl.BlockSpec((n_pieces, rows, part), lambda i, half: (0, 0, i)),
            scratch_shapes=[pltpu.VMEM((total, inner), BF16)] * 2,
        ),
        out_shape=jax.ShapeDtypeStruct((n_pieces, rows, segments * part), F32),
        compiler_params=pltpu.CompilerParams(vmem_limit_bytes=VMEM_LIMIT),
        cost_estimate=pl.CostEstimate(
            flops=6 * total * inner * segments * part,
            bytes_accessed=4 * (total * inner + segments * part * (inner + total)),
            transcendentals=0,
        ),
        name="ladder",
    )(half, *pieces, coupling)


def pick_kernel(n_pieces, place_ref, segment_ref, factor_ref, *refs):
    pieces, out_ref = refs[:-1], refs[-1]
    slots = place_ref.shape[0]
    width = out_ref.shape[-1]
    picked = jnp.zeros((slots, pieces[0].shape[1]), F32)
    base = 0
    for first in range(0, len(pieces), n_pieces):
        block = jnp.concatenate([piece[...] for piece in pieces[first : first + n_pieces]], axis=0)
        high, low = halves(block)
        lanes = lax.broadcasted_iota(jnp.int32, (slots, block.shape[0]), 1) + base
        chosen = jnp.where(lanes == place_ref[...], 1.0, 0.0).astype(BF16)
        nn = ((1,), (0,))
        picked += dot(chosen, high, nn) + dot(chosen, low, nn)
        base += block.shape[0]
    value = picked[:, :width]
    for segment in range(1, picked.shape[1] // width):
        value = jnp.where(segment_ref[...] == segment, picked[:, segment * width : (segment + 1) * width], value)
    out_ref[...] = (value * factor_ref[...]).reshape(out_ref.shape)


def pick(place, segment, factor, chunks, width):
    n_pieces = len(chunks[0])
    pieces = [piece for chunk in chunks for piece in chunk]
    slots = place.shape[0]
    inner = pieces[0].shape[1]
    rows = sum(piece.shape[0] for piece in pieces)
    return pl.pallas_call(
        functools.partial(pick_kernel, n_pieces),
        out_shape=jax.ShapeDtypeStruct((n_pieces, slots // n_pieces, width), F32),
        compiler_params=pltpu.CompilerParams(vmem_limit_bytes=VMEM_LIMIT),
        cost_estimate=pl.CostEstimate(
            flops=4 * slots * rows * inner, bytes_accessed=4 * rows * inner, transcendentals=0
        ),
        name="pick",
    )(place, segment, factor, *pieces)


def mix_kernel(matrix_ref, *refs):
    pieces, out_ref = refs[:-1], refs[-1]
    high, low = halves(jnp.concatenate([piece[...] for piece in pieces], axis=0))
    matrix_high, matrix_low = halves(matrix_ref[...])
    nn = ((1,), (0,))
    value = dot(high, matrix_high, nn)
    value += dot(low, matrix_high, nn) + dot(high, matrix_low, nn)
    out_ref[...] = value.reshape(out_ref.shape)


def mix(matrix, pieces):
    n_pieces = len(pieces)
    rows, width = pieces[0].shape
    block = 256
    return pl.pallas_call(
        mix_kernel,
        grid=(width // block,),
        in_specs=[pl.BlockSpec((width, block), lambda i: (0, i))]
        + [pl.BlockSpec((rows, width), lambda i: (0, 0))] * n_pieces,
        out_specs=pl.BlockSpec((n_pieces, rows, block), lambda i: (0, 0, i)),
        out_shape=jax.ShapeDtypeStruct((n_pieces, rows, width), F32),
        compiler_params=pltpu.CompilerParams(vmem_limit_bytes=VMEM_LIMIT),
        cost_estimate=pl.CostEstimate(
            flops=6 * n_pieces * rows * width * width,
            bytes_accessed=4 * (width * width + 2 * n_pieces * rows * width),
            transcendentals=0,
        ),
        name="mix",
    )(matrix, *pieces)


def combine_kernel(n_parts, rows, offset, own, count, where_ref, *refs):
    parts = refs[:n_parts]
    loads = refs[n_parts:-2]
    keep_ref, send_ref = refs[-2:]
    segments = pl.num_programs(0)
    z, core = where_ref[0], where_ref[1]
    segment = pl.program_id(0)
    value = parts[0][...].reshape(2 * rows, -1)
    for part in parts[1:]:
        value += part[...].reshape(2 * rows, -1)
    line = lax.broadcasted_iota(jnp.int32, (2 * rows, 1), 0)
    second = (line >= rows).astype(jnp.int32)
    inside = line - second * rows + offset
    hole = z * (2 * own) + second * own + inside
    wanted = jnp.where(inside < own, hole * segments + segment, -1)
    for load in loads:
        for first in range(0, load.shape[0], count + 8):
            named = load[first + count : first + count + 1, :count].astype(jnp.int32)
            chosen = jnp.where(wanted == named, 1.0, 0.0).astype(BF16)
            high, low = halves(load[first : first + count, :])
            nn = ((1,), (0,))
            value += dot(chosen, high, nn) + dot(chosen, low, nn)
    top, bottom = value[:rows], value[rows:]
    keep_ref[...] = jnp.where(core == 0, top, bottom)
    send_ref[...] = jnp.where(core == 0, bottom, top)


def combine(where, parts, loads, rows, offset, own, count):
    width = parts[0].shape[-1]
    part = loads[0].shape[1]
    segments = width // part
    height = loads[0].shape[0]
    out = jax.ShapeDtypeStruct((rows, width), F32)
    return pl.pallas_call(
        functools.partial(combine_kernel, len(parts), rows, offset, own, count),
        grid_spec=pltpu.PrefetchScalarGridSpec(
            num_scalar_prefetch=1,
            grid=(segments,),
            in_specs=[pl.BlockSpec((2 * rows, part), lambda i, where: (0, i))] * len(parts)
            + [pl.BlockSpec((height, part), lambda i, where: (0, 0))] * len(loads),
            out_specs=[pl.BlockSpec((rows, part), lambda i, where: (0, i))] * 2,
        ),
        out_shape=[out, out],
        compiler_params=pltpu.CompilerParams(vmem_limit_bytes=VMEM_LIMIT),
        cost_estimate=pl.CostEstimate(
            flops=8 * rows * width * height * len(loads),
            bytes_accessed=4 * (2 * rows * width * (len(parts) + 1) + height * part * len(loads)),
            transcendentals=0,
        ),
        name="combine",
    )(where, *parts, *loads)


def update_kernel(offsets, core_ref, driving_ref, denominator_ref, *refs):
    out_ref = refs[-1]
    own = out_ref.shape[0]
    mine = pl.program_id(0) % 2 == core_ref[0]
    for number, offset in enumerate(offsets):
        kept, received = refs[2 * number], refs[2 * number + 1]
        size = min(kept.shape[0], own - offset)
        lines = slice(offset, offset + size)
        value = jnp.where(mine, kept[:size, :], received[:size, :])
        out_ref[lines, :] = (driving_ref[lines, :] + value) / denominator_ref[lines, :]


def update(core, driving, denominator, sums, offsets, part):
    own, width = driving.shape
    whole = pl.BlockSpec((own, part), lambda i, core: (0, i))
    flat = [piece for pair in sums for piece in pair]
    return pl.pallas_call(
        functools.partial(update_kernel, offsets),
        grid_spec=pltpu.PrefetchScalarGridSpec(
            num_scalar_prefetch=1,
            grid=(width // part,),
            in_specs=[whole, whole]
            + [pl.BlockSpec((piece.shape[0], part), lambda i, core: (0, i // 2)) for piece in flat],
            out_specs=whole,
        ),
        out_shape=jax.ShapeDtypeStruct((own, width), F32),
        compiler_params=pltpu.CompilerParams(vmem_limit_bytes=VMEM_LIMIT),
        cost_estimate=pl.CostEstimate(flops=2 * own * width, bytes_accessed=16 * own * width, transcendentals=0),
        name="update",
    )(core, driving, denominator, *flat)


def on_device(
    amplitude,
    ladder_coupling,
    crossed_coupling,
    channel_slot,
    channel_of,
    source_row,
    target_row,
    recoupling,
    driving,
    denominator,
):
    groups = lax.axis_size("row")
    columns = lax.axis_size("col")
    depth = columns // 2
    r = lax.axis_index("row")
    c = lax.axis_index("col")
    z, core = c // 2, c % 2
    inner = amplitude.shape[1]
    own = driving.shape[0]
    width = crossed_coupling.shape[1]
    part = width // 2
    count = source_row.shape[1]
    assert depth == groups and amplitude.shape[0] == 2 * own

    across = [[(i, i ^ k) for i in range(groups)] for k in range(1, groups)]
    swap = [(i, i ^ 1) for i in range(columns)]

    def at(array, index):
        return lax.dynamic_index_in_dim(array, index, 0, keepdims=False)

    padded = -(-own // 4) * 4
    sizes = chunk_sizes(padded)
    offsets = [sum(sizes[:k]) for k in range(len(sizes))]
    pairs = jnp.pad(amplitude.reshape(2, own, inner), ((0, 0), (0, padded - own), (0, 0)))
    chunks = []
    for size, offset in zip(sizes, offsets):
        local = pairs[:, offset : offset + size].reshape(2 * size, inner)
        chunks.append([local] + [lax.ppermute(local, "row", perm) for perm in across])

    reduced = []
    for size, pieces in zip(sizes, chunks):
        sent = ladder((1 - core)[None], pieces, ladder_coupling, width)
        received = lax.ppermute(sent, "col", swap)
        kept = ladder(core[None], pieces, ladder_coupling, width)

        def own_sum(owner):
            place = jnp.clip(owner, 0, depth - 1) ^ r
            return at(kept, place) + at(received, place)

        right, left = None, None
        for step in range(depth - 1):
            to_right = own_sum(depth - 1 - step + z)
            to_left = own_sum(z - (depth - 1) + step)
            if step:
                to_right, to_left = to_right + right, to_left + left
            up = [(i, i + 2) for i in range(columns - 2) if i // 2 <= step]
            down = [(columns - 1 - i, columns - 1 - j) for i, j in up]
            right = lax.ppermute(to_right, "col", up)
            left = lax.ppermute(to_left, "col", down)
        reduced.append((own_sum(z), right, left))

    owners = channel_slot[channel_of[0, :, 0]]
    onehot = (owners[:, None] == jnp.arange(groups, dtype=jnp.int32)[None, :]).astype(jnp.int32)
    before = jnp.cumsum(onehot, axis=0) - onehot
    slot = owners * CAP + jnp.sum(before * onehot, axis=1)
    in_slot = slot[None, :] == jnp.arange(groups * CAP, dtype=jnp.int32)[:, None]
    used = jnp.any(in_slot, axis=1)
    source = jnp.sum(jnp.where(in_slot, source_row, 0), axis=1)
    factor = jnp.sum(jnp.where(in_slot, recoupling, 0.0), axis=1)
    per_row = inner // width
    hole, segment = source // per_row, source % per_row
    place = jnp.full_like(hole, -1)
    for size, offset in zip(sizes, offsets):
        inside = hole % own - offset
        spot = 2 * groups * offset + ((hole // (2 * own)) ^ r) * 2 * size + (hole // own % 2) * size + inside
        place = jnp.where((inside >= 0) & (inside < size), spot, place)
    place = jnp.where(used, place, -1)
    picked = pick(place[:, None], segment[:, None], factor[:, None], chunks, width)
    arrived = [at(picked, r)] + [lax.ppermute(at(picked, r ^ k), "row", across[k - 1]) for k in range(1, groups)]
    product = mix(crossed_coupling[0], arrived)
    returned = [product[0]] + [lax.ppermute(product[k], "row", across[k - 1]) for k in range(1, groups)]
    returned = jnp.concatenate(returned, axis=0)
    crossed = returned[((slot // CAP) ^ r) * CAP + slot % CAP]

    names = jnp.pad(target_row[:1].astype(F32), ((0, 7), (0, part - count)))
    first = jnp.concatenate([crossed[:, :part], names], axis=0)
    second = jnp.concatenate([crossed[:, part:], names], axis=0)
    to_keep = jnp.where(core == 0, first, second)
    to_send = jnp.where(core == 0, second, first)
    load = jnp.concatenate([to_keep, lax.ppermute(to_send, "col", swap)], axis=0)
    right, left = [load], [load]
    for step in range(depth - 1):
        up = [(i, i + 2) for i in range(columns - 2) if i // 2 >= step]
        down = [(columns - 1 - i, columns - 1 - j) for i, j in up]
        right.append(lax.ppermute(right[-1], "col", up))
        left.append(lax.ppermute(left[-1], "col", down))
    loads = [load] + [right[k] + left[depth - k] for k in range(1, depth)]

    where = jnp.stack([z, core]).astype(jnp.int32)
    sums = []
    for size, offset, parts in zip(sizes, offsets, reduced):
        keep, send = combine(where, parts, loads, size, offset, own, count)
        sums.append((keep, lax.ppermute(send, "col", swap)))
    return update(core[None], driving, denominator, sums, offsets, part)


def solution(mesh):
    in_specs = (
        P("row", "col"),
        P("row", "col"),
        P("row", None, None),
        P(),
        P("col", "row", None),
        P("col", "row"),
        P("col", "row"),
        P("col", "row"),
        P("col", "row"),
        P("col", "row"),
    )
    out_specs = P("col", "row")
    return jax.shard_map(
        on_device, mesh=mesh, in_specs=in_specs, out_specs=out_specs, check_vma=False
    )
```

```python
import functools

import jax
import jax.numpy as jnp
from jax import lax
from jax.experimental import pallas as pl
from jax.experimental.pallas import tpu as pltpu
from jax.sharding import PartitionSpec as P

CAP = 40
F32 = jnp.float32
BF16 = jnp.bfloat16
VMEM_LIMIT = 56 * 1024 * 1024


def chunk_sizes(total):
    sizes = [32, 32, 36]
    return sizes if sum(sizes) == total else [24, total - 24]


def halves(x):
    high = x.astype(BF16)
    return high, (x - high.astype(F32)).astype(BF16)


def dot(x, y, contract):
    return lax.dot_general(x, y, ((contract[0], contract[1]), ((), ())), preferred_element_type=F32)


def ladder_kernel(n_pieces, where_ref, *refs):
    pieces = refs[:n_pieces]
    coupling_ref, *received, out_ref, amplitude_ref = refs[n_pieces:]
    groups, rows = out_ref.shape[:2]
    total = groups * rows
    gap = amplitude_ref.shape[1] // 2

    @pl.when(pl.program_id(0) == 0)
    def _():
        high, low = halves(jnp.concatenate([piece[...] for piece in pieces], axis=0).T)
        amplitude_ref[:, :total] = high
        amplitude_ref[:, gap : gap + total] = low

    coupling_high, coupling_low = halves(coupling_ref[...])
    nn = ((1,), (0,))
    both = dot(coupling_high, amplitude_ref[...], nn)
    value = both[:, :total] + both[:, gap : gap + total] + dot(coupling_low, amplitude_ref[:, :total], nn)
    value = value.T
    for k in range(groups):
        piece = value[k * rows : (k + 1) * rows]
        line = k ^ where_ref[0]
        out_ref[line] = piece + received[0][line] if received else piece


def ladder(where, pieces, coupling, width, received=None):
    rows, inner = pieces[0].shape
    total = sum(piece.shape[0] for piece in pieces)
    groups = total // rows
    part = width // 2
    segments = coupling.shape[0] // width
    block = pl.BlockSpec((groups, rows, part), lambda i, where: (0, 0, i))
    extra = [] if received is None else [received]
    return pl.pallas_call(
        functools.partial(ladder_kernel, len(pieces)),
        grid_spec=pltpu.PrefetchScalarGridSpec(
            num_scalar_prefetch=1,
            grid=(segments,),
            in_specs=[pl.BlockSpec(piece.shape, lambda i, where: (0, 0)) for piece in pieces]
            + [pl.BlockSpec((part, inner), lambda i, where: (2 * i + where[1], 0))]
            + [block] * len(extra),
            out_specs=block,
            scratch_shapes=[pltpu.VMEM((inner, 2 * (-(-total // 128) * 128)), BF16)],
        ),
        out_shape=jax.ShapeDtypeStruct((groups, rows, segments * part), F32),
        compiler_params=pltpu.CompilerParams(vmem_limit_bytes=VMEM_LIMIT),
        cost_estimate=pl.CostEstimate(
            flops=total * inner * segments * part,
            bytes_accessed=part * inner,
            transcendentals=0,
        ),
        name="ladder",
    )(where, *pieces, coupling, *extra)


def pick_kernel(counts, place_ref, segment_ref, factor_ref, *refs):
    pieces, out_ref = refs[:-1], refs[-1]
    slots = place_ref.shape[0]
    width = out_ref.shape[-1]
    picked = jnp.zeros((slots, pieces[0].shape[1]), F32)
    base = 0
    first = 0
    for number in counts:
        block = jnp.concatenate([piece[...] for piece in pieces[first : first + number]], axis=0)
        first += number
        high, low = halves(block)
        lanes = lax.broadcasted_iota(jnp.int32, (slots, block.shape[0]), 1) + base
        chosen = jnp.where(lanes == place_ref[...], 1.0, 0.0).astype(BF16)
        nn = ((1,), (0,))
        picked += dot(chosen, high, nn) + dot(chosen, low, nn)
        base += block.shape[0]
    value = picked[:, :width]
    for segment in range(1, picked.shape[1] // width):
        value = jnp.where(segment_ref[...] == segment, picked[:, segment * width : (segment + 1) * width], value)
    out_ref[...] = (value * factor_ref[...]).reshape(out_ref.shape)


def pick(place, segment, factor, chunks, groups, width):
    pieces = [piece for chunk in chunks for piece in chunk]
    slots = place.shape[0]
    return pl.pallas_call(
        functools.partial(pick_kernel, [len(chunk) for chunk in chunks]),
        out_shape=jax.ShapeDtypeStruct((groups, slots // groups, width), F32),
        compiler_params=pltpu.CompilerParams(vmem_limit_bytes=VMEM_LIMIT),
        cost_estimate=pl.CostEstimate(flops=slots * width, bytes_accessed=slots * width, transcendentals=0),
        name="pick",
    )(place, segment, factor, *pieces)


def mix_kernel(matrix_ref, *refs):
    pieces, out_ref = refs[:-1], refs[-1]
    high, low = halves(jnp.concatenate([piece[...] for piece in pieces], axis=0))
    matrix_high, matrix_low = halves(matrix_ref[...])
    nn = ((1,), (0,))
    value = dot(high, matrix_high, nn)
    value += dot(low, matrix_high, nn) + dot(high, matrix_low, nn)
    out_ref[...] = value.reshape(out_ref.shape)


def mix(matrix, pieces):
    n_pieces = len(pieces)
    rows, width = pieces[0].shape
    block = 256
    return pl.pallas_call(
        mix_kernel,
        grid=(width // block,),
        in_specs=[pl.BlockSpec((width, block), lambda i: (0, i))]
        + [pl.BlockSpec((rows, width), lambda i: (0, 0))] * n_pieces,
        out_specs=pl.BlockSpec((n_pieces, rows, block), lambda i: (0, 0, i)),
        out_shape=jax.ShapeDtypeStruct((n_pieces, rows, width), F32),
        compiler_params=pltpu.CompilerParams(vmem_limit_bytes=VMEM_LIMIT),
        cost_estimate=pl.CostEstimate(
            flops=6 * n_pieces * rows * width * width,
            bytes_accessed=4 * (width * width + 2 * n_pieces * rows * width),
            transcendentals=0,
        ),
        name="mix",
    )(matrix, *pieces)


def spread_kernel(count, holes_ref, *refs):
    loads = refs[:-3]
    pairs = [loads[:1]] + [loads[k : k + 2] for k in range(1, len(loads), 2)]
    out_ref, high_ref, low_ref = refs[-3:]
    segments = pl.num_programs(0)
    segment = pl.program_id(0)
    spans = [(pair, first) for pair in pairs for first in range(0, pair[0].shape[0], count + 8)]

    @pl.when(segment == 0)
    def _():
        for number, (pair, first) in enumerate(spans):
            high, low = halves(sum(load[first : first + count, :] for load in pair))
            high_ref[number * count : (number + 1) * count, :] = high
            low_ref[number * count : (number + 1) * count, :] = low

    wanted = jnp.where(holes_ref[...] >= 0, holes_ref[...] * segments + segment, -1)
    chosen = []
    for pair, first in spans:
        named = sum(load[first + count : first + count + 1, :count] for load in pair).astype(jnp.int32)
        chosen.append(jnp.where(wanted == named, 1.0, 0.0))
    chosen = jnp.concatenate(chosen, axis=1).astype(BF16)
    nn = ((1,), (0,))
    out_ref[...] = dot(chosen, high_ref[...], nn) + dot(chosen, low_ref[...], nn)


def spread(holes, loads, segments, count):
    rows = holes.shape[0]
    height, part = loads[0].shape
    held = (len(loads) + 1) // 2 * (height // (count + 8)) * count
    return pl.pallas_call(
        functools.partial(spread_kernel, count),
        grid=(segments,),
        in_specs=[pl.BlockSpec((rows, 1), lambda i: (0, 0))]
        + [pl.BlockSpec((height, part), lambda i: (0, 0))] * len(loads),
        out_specs=pl.BlockSpec((rows, part), lambda i: (0, i)),
        out_shape=jax.ShapeDtypeStruct((rows, segments * part), F32),
        scratch_shapes=[pltpu.VMEM((held, part), BF16)] * 2,
        compiler_params=pltpu.CompilerParams(vmem_limit_bytes=VMEM_LIMIT),
        cost_estimate=pl.CostEstimate(
            flops=rows * segments * part,
            bytes_accessed=rows * segments * part,
            transcendentals=0,
        ),
        name="spread",
    )(holes, *loads)


def update_kernel(core_ref, driving_ref, denominator_ref, kept_ref, received_ref, *refs):
    out_ref = refs[-1]
    part = kept_ref.shape[1]
    for half in range(2):
        lanes = slice(half * part, (half + 1) * part)
        value = jnp.where(core_ref[0] == half, kept_ref[...], received_ref[...])
        out_ref[:, lanes] = (driving_ref[:, lanes] + value) / denominator_ref[:, lanes]


def update(core, target, driving, denominator, kept, received, offset, part):
    own, width = driving.shape
    size = min(kept.shape[0], own - offset)
    tile = next(rows for rows in (32, 16, 8) if offset % rows == 0 and rows <= size)
    lines = pl.BlockSpec((tile, 2 * part), lambda i, j, core: (offset // tile + i, j))
    half = pl.BlockSpec((tile, part), lambda i, j, core: (i, j))
    return pl.pallas_call(
        update_kernel,
        grid_spec=pltpu.PrefetchScalarGridSpec(
            num_scalar_prefetch=1,
            grid=(pl.cdiv(size, tile), width // (2 * part)),
            in_specs=[lines, lines, half, half] + [pl.BlockSpec(memory_space=pl.ANY)] * len(target),
            out_specs=lines,
        ),
        out_shape=jax.ShapeDtypeStruct((own, width), F32),
        input_output_aliases={5: 0} if target else {},
        compiler_params=pltpu.CompilerParams(vmem_limit_bytes=VMEM_LIMIT),
        cost_estimate=pl.CostEstimate(flops=size * width, bytes_accessed=size * width, transcendentals=0),
        name="update",
    )(core, driving, denominator, kept, received, *target)


def on_device(
    amplitude,
    ladder_coupling,
    crossed_coupling,
    channel_slot,
    channel_of,
    source_row,
    target_row,
    recoupling,
    driving,
    denominator,
):
    groups = lax.axis_size("row")
    columns = lax.axis_size("col")
    depth = columns // 2
    r = lax.axis_index("row")
    c = lax.axis_index("col")
    z, core = c // 2, c % 2
    inner = amplitude.shape[1]
    own = driving.shape[0]
    width = crossed_coupling.shape[1]
    part = width // 2
    count = source_row.shape[1]
    assert depth == groups and amplitude.shape[0] == 2 * own

    across = [[(i, i ^ k) for i in range(groups)] for k in range(1, groups)]
    swap = [(i, i ^ 1) for i in range(columns)]

    def at(array, index):
        return lax.dynamic_index_in_dim(array, index, 0, keepdims=False)

    padded = -(-own // 4) * 4
    sizes = chunk_sizes(padded)
    offsets = [sum(sizes[:k]) for k in range(len(sizes))]
    pairs = jnp.pad(amplitude.reshape(2, own, inner), ((0, 0), (0, padded - own), (0, 0)))
    locals_ = [
        pairs[:, offset : offset + size].reshape(2 * size, inner) for size, offset in zip(sizes, offsets)
    ]

    def spread_first(local, whole):
        return [local] + [lax.ppermute(local, "row", perm) for perm in (across if whole else across[:2])]

    def spread_rest(pieces):
        if len(pieces) == groups:
            return pieces
        cut = pieces[0].shape[0] // 16 * 8
        top = lax.ppermute(pieces[2][:cut], "row", across[0])
        bottom = lax.ppermute(pieces[1][cut:], "row", across[1])
        return [*pieces, top, bottom]

    def tie(*arrays):
        return lax.optimization_barrier(arrays)

    owners = channel_slot[channel_of[0, :, 0]]
    onehot = (owners[:, None] == jnp.arange(groups, dtype=jnp.int32)[None, :]).astype(jnp.int32)
    before = jnp.cumsum(onehot, axis=0) - onehot
    slot = owners * CAP + jnp.sum(before * onehot, axis=1)
    in_slot = slot[None, :] == jnp.arange(groups * CAP, dtype=jnp.int32)[:, None]
    used = jnp.any(in_slot, axis=1)
    source = jnp.sum(jnp.where(in_slot, source_row, 0), axis=1)
    factor = jnp.sum(jnp.where(in_slot, recoupling, 0.0), axis=1)
    per_row = inner // width
    hole, segment = source // per_row, source % per_row
    place = jnp.full_like(hole, -1)
    for size, offset in zip(sizes, offsets):
        inside = hole % own - offset
        spot = 2 * groups * offset + ((hole // (2 * own)) ^ r) * 2 * size + (hole // own % 2) * size + inside
        place = jnp.where((inside >= 0) & (inside < size), spot, place)
    place = jnp.where(used, place, -1)
    names = jnp.pad(target_row[:1].astype(F32), ((0, 7), (0, part - count)))

    last = len(sizes) - 1
    square = groups == 4
    chunks = [spread_rest(spread_first(locals_[0], not square))]
    theirs = jnp.stack([r, 1 - core]).astype(jnp.int32)
    ours = jnp.stack([r, core]).astype(jnp.int32)
    place, segment, factor, names, theirs, ours, *locals_ = tie(
        place[:, None], segment[:, None], factor[:, None], names, theirs, ours, *locals_
    )
    theirs, *chunks[0] = tie(theirs, *chunks[0])

    def gather_chunks():
        held = None
        for kernel in range(last + 1):
            rest = [] if held is None else spread_rest(held)
            first = spread_first(locals_[kernel + 1], not square) if kernel < last else []
            flight = yield None, rest + first
            if rest:
                chunks.append(flight[: len(rest)])
            held = flight[len(rest) :]

    loads = []

    def exchange_segments():
        picked = pick(place, segment, factor, chunks, groups, width)
        arrived = yield picked, [at(picked, r)] + [
            lax.ppermute(at(picked, r ^ k), "row", across[k - 1]) for k in range(1, groups)
        ]
        product = mix(crossed_coupling[0], arrived)
        returned = yield product, [product[0]] + [
            lax.ppermute(product[k], "row", across[k - 1]) for k in range(1, groups)
        ]
        crossed = jnp.concatenate(returned, axis=0)[((slot // CAP) ^ r) * CAP + slot % CAP]
        first = jnp.concatenate([crossed[:, :part], names], axis=0)
        second = jnp.concatenate([crossed[:, part:], names], axis=0)
        to_keep = jnp.where(core == 0, first, second)
        to_send = jnp.where(core == 0, second, first)
        load = jnp.concatenate([to_keep, lax.ppermute(to_send, "col", swap)], axis=0)
        right, left = [load], [load]
        for step in range(depth - 1):
            up = [(i, i + 2) for i in range(columns - 2) if i // 2 >= step]
            down = [(columns - 1 - i, columns - 1 - j) for i, j in up]
            flight = [lax.ppermute(right[-1], "col", up), lax.ppermute(left[-1], "col", down)]
            moved = yield load, flight
            right.append(moved[0])
            left.append(moved[1])
        loads.append(load)
        for k in range(1, depth):
            loads.extend([right[k], left[depth - k]])

    holes = []
    for size, offset in zip(sizes, offsets):
        inside = jnp.tile(jnp.arange(size, dtype=jnp.int32) + offset, 2)
        second = jnp.repeat(jnp.arange(2, dtype=jnp.int32), size)
        holes.append(jnp.where(inside < own, (2 * z + second) * own + inside, -1))
    holes = jnp.concatenate(holes)[:, None]

    lines = [list(range(k, columns, 2)) for k in (0, 1)]
    reduced = {}

    def scatter_line(number, value):
        reduced[number] = lax.psum_scatter(
            value.reshape(depth * 2 * sizes[number], -1),
            "col",
            scatter_dimension=0,
            axis_index_groups=lines,
            tiled=True,
        )

    def walk_line(number, value):
        def own_sum(owner):
            return at(value, jnp.clip(owner, 0, depth - 1))

        right, left = None, None
        for step in range(depth - 1):
            to_right, to_left = own_sum(depth - 1 - step + z), own_sum(z - (depth - 1) + step)
            if step:
                to_right, to_left = to_right + right, to_left + left
            up = [(i, i + 2) for i in range(columns - 2) if i // 2 <= step]
            down = [(columns - 1 - i, columns - 1 - j) for i, j in up]
            right, left = yield None, [lax.ppermute(to_right, "col", up), lax.ppermute(to_left, "col", down)]
        reduced[number] = own_sum(z) + right + left

    gathering, exchanging = gather_chunks(), exchange_segments()
    walks, sent = [], None
    moved = {}

    def begin(stage):
        try:
            return stage.send(moved.pop(stage, None))
        except StopIteration:
            return None, None

    for kernel in range(2 * len(sizes)):
        number, keeping = kernel // 2, kernel % 2
        token, after = (ours, theirs) if keeping else (theirs, ours)
        stages = []
        if kernel < last:
            locals_[kernel + 1], token = tie(locals_[kernel + 1], token)
        if kernel <= last:
            stages.append(gathering)
        else:
            stages.append(exchanging)
        stages += walks
        flights = {}
        for stage in stages:
            ahead, flight = begin(stage)
            if ahead is not None:
                ahead, token = tie(ahead, token)
            if flight is not None:
                flights[stage] = flight
        if keeping:
            received = lax.ppermute(sent, "col", swap)
            value = ladder(token, chunks[number], ladder_coupling, width, received)
        else:
            value = ladder(token, chunks[number], ladder_coupling, width)
        flat = [array for flight in flights.values() for array in flight]
        value, after, *flat = tie(value, after, *flat)
        for stage, flight in flights.items():
            moved[stage], flat = flat[: len(flight)], flat[len(flight) :]
        if kernel == last:
            chunks.append(moved.pop(gathering))
        if not keeping:
            ours, sent = after, value
            continue
        theirs = after
        if number - 1 in reduced:
            value, reduced[number - 1] = tie(value, reduced[number - 1])
        if number < 2:
            scatter_line(number, value)
        else:
            walks.append(walk_line(number, value))
    while len(reduced) < len(sizes) or not loads:
        flights = {stage: begin(stage)[1] for stage in [exchanging] * (not loads) + walks}
        flights = {stage: flight for stage, flight in flights.items() if flight is not None}
        flat = [array for flight in flights.values() for array in flight]
        flat = list(tie(*flat)) if flat else []
        for stage, flight in flights.items():
            moved[stage], flat = flat[: len(flight)], flat[len(flight) :]
    added = spread(holes, loads, ladder_coupling.shape[0] // width, count)

    out = []
    for number, (size, offset) in enumerate(zip(sizes, offsets)):
        line = reduced[number]
        if number == last:
            line, *out = tie(line, *out)
        line = (line + added[2 * offset : 2 * (offset + size)]).reshape(2, size, -1)
        received = lax.ppermute(at(line, 1 - core), "col", swap)
        out = [update(core[None], out, driving, denominator, at(line, core), received, offset, part)]
    return out[0]


def solution(mesh):
    in_specs = (
        P("row", "col"),
        P("row", "col"),
        P("row", None, None),
        P(),
        P("col", "row", None),
        P("col", "row"),
        P("col", "row"),
        P("col", "row"),
        P("col", "row"),
        P("col", "row"),
    )
    out_specs = P("col", "row")
    return jax.shard_map(
        on_device, mesh=mesh, in_specs=in_specs, out_specs=out_specs, check_vma=False
    )
```

```python
import functools

import jax
import jax.numpy as jnp
from jax import lax
from jax.experimental import pallas as pl
from jax.experimental.pallas import tpu as pltpu
from jax.sharding import PartitionSpec as P

CAP = 40
F32 = jnp.float32
BF16 = jnp.bfloat16
VMEM_LIMIT = 56 * 1024 * 1024


def chunk_sizes(total):
    sizes = [32, 32, 36]
    return sizes if sum(sizes) == total else [24, total - 24]


def halves(x):
    high = x.astype(BF16)
    return high, (x - high.astype(F32)).astype(BF16)


def dot(x, y, contract):
    return lax.dot_general(x, y, ((contract[0], contract[1]), ((), ())), preferred_element_type=F32)


def ladder_kernel(n_pieces, where_ref, *refs):
    pieces = refs[:n_pieces]
    coupling_ref, *received, out_ref, amplitude_ref = refs[n_pieces:]
    groups, rows = out_ref.shape[:2]
    total = groups * rows
    gap = amplitude_ref.shape[1] // 2

    @pl.when(pl.program_id(0) == 0)
    def _():
        high, low = halves(jnp.concatenate([piece[...] for piece in pieces], axis=0).T)
        amplitude_ref[:, :total] = high
        amplitude_ref[:, gap : gap + total] = low

    coupling_high, coupling_low = halves(coupling_ref[...])
    nn = ((1,), (0,))
    both = dot(coupling_high, amplitude_ref[...], nn)
    value = both[:, :total] + both[:, gap : gap + total] + dot(coupling_low, amplitude_ref[:, :total], nn)
    value = value.T
    for k in range(groups):
        piece = value[k * rows : (k + 1) * rows]
        line = k ^ where_ref[0]
        out_ref[line] = piece + received[0][line] if received else piece


def ladder(where, pieces, coupling, width, received=None):
    rows, inner = pieces[0].shape
    total = sum(piece.shape[0] for piece in pieces)
    groups = total // rows
    part = width // 2
    segments = coupling.shape[0] // width
    block = pl.BlockSpec((groups, rows, part), lambda i, where: (0, 0, i))
    extra = [] if received is None else [received]
    return pl.pallas_call(
        functools.partial(ladder_kernel, len(pieces)),
        grid_spec=pltpu.PrefetchScalarGridSpec(
            num_scalar_prefetch=1,
            grid=(segments,),
            in_specs=[pl.BlockSpec(piece.shape, lambda i, where: (0, 0)) for piece in pieces]
            + [pl.BlockSpec((part, inner), lambda i, where: (2 * i + where[1], 0))]
            + [block] * len(extra),
            out_specs=block,
            scratch_shapes=[pltpu.VMEM((inner, 2 * (-(-total // 128) * 128)), BF16)],
        ),
        out_shape=jax.ShapeDtypeStruct((groups, rows, segments * part), F32),
        compiler_params=pltpu.CompilerParams(vmem_limit_bytes=VMEM_LIMIT),
        cost_estimate=pl.CostEstimate(
            flops=total * inner * segments * part,
            bytes_accessed=part * inner,
            transcendentals=0,
        ),
        name="ladder",
    )(where, *pieces, coupling, *extra)


def pick_kernel(counts, place_ref, segment_ref, factor_ref, *refs):
    pieces, out_ref = refs[:-1], refs[-1]
    slots = place_ref.shape[0]
    width = out_ref.shape[-1]
    picked = jnp.zeros((slots, pieces[0].shape[1]), F32)
    base = 0
    first = 0
    for number in counts:
        block = jnp.concatenate([piece[...] for piece in pieces[first : first + number]], axis=0)
        first += number
        high, low = halves(block)
        lanes = lax.broadcasted_iota(jnp.int32, (slots, block.shape[0]), 1) + base
        chosen = jnp.where(lanes == place_ref[...], 1.0, 0.0).astype(BF16)
        nn = ((1,), (0,))
        picked += dot(chosen, high, nn) + dot(chosen, low, nn)
        base += block.shape[0]
    value = picked[:, :width]
    for segment in range(1, picked.shape[1] // width):
        value = jnp.where(segment_ref[...] == segment, picked[:, segment * width : (segment + 1) * width], value)
    out_ref[...] = (value * factor_ref[...]).reshape(out_ref.shape)


def pick(place, segment, factor, chunks, groups, width):
    pieces = [piece for chunk in chunks for piece in chunk]
    slots = place.shape[0]
    return pl.pallas_call(
        functools.partial(pick_kernel, [len(chunk) for chunk in chunks]),
        out_shape=jax.ShapeDtypeStruct((groups, slots // groups, width), F32),
        compiler_params=pltpu.CompilerParams(vmem_limit_bytes=VMEM_LIMIT),
        cost_estimate=pl.CostEstimate(flops=slots * width, bytes_accessed=slots * width, transcendentals=0),
        name="pick",
    )(place, segment, factor, *pieces)


def mix_kernel(matrix_ref, *refs):
    pieces, out_ref = refs[:-1], refs[-1]
    high, low = halves(jnp.concatenate([piece[...] for piece in pieces], axis=0))
    matrix_high, matrix_low = halves(matrix_ref[...])
    nn = ((1,), (0,))
    value = dot(high, matrix_high, nn)
    value += dot(low, matrix_high, nn) + dot(high, matrix_low, nn)
    out_ref[...] = value.reshape(out_ref.shape)


def mix(matrix, pieces):
    n_pieces = len(pieces)
    rows, width = pieces[0].shape
    block = 256
    return pl.pallas_call(
        mix_kernel,
        grid=(width // block,),
        in_specs=[pl.BlockSpec((width, block), lambda i: (0, i))]
        + [pl.BlockSpec((rows, width), lambda i: (0, 0))] * n_pieces,
        out_specs=pl.BlockSpec((n_pieces, rows, block), lambda i: (0, 0, i)),
        out_shape=jax.ShapeDtypeStruct((n_pieces, rows, width), F32),
        compiler_params=pltpu.CompilerParams(vmem_limit_bytes=VMEM_LIMIT),
        cost_estimate=pl.CostEstimate(
            flops=6 * n_pieces * rows * width * width,
            bytes_accessed=4 * (width * width + 2 * n_pieces * rows * width),
            transcendentals=0,
        ),
        name="mix",
    )(matrix, *pieces)


def spread_kernel(count, holes_ref, *refs):
    loads = refs[:-3]
    pairs = [loads[:1]] + [loads[k : k + 2] for k in range(1, len(loads), 2)]
    out_ref, high_ref, low_ref = refs[-3:]
    segments = pl.num_programs(0)
    segment = pl.program_id(0)
    spans = [(pair, first) for pair in pairs for first in range(0, pair[0].shape[0], count + 8)]

    @pl.when(segment == 0)
    def _():
        for number, (pair, first) in enumerate(spans):
            high, low = halves(sum(load[first : first + count, :] for load in pair))
            high_ref[number * count : (number + 1) * count, :] = high
            low_ref[number * count : (number + 1) * count, :] = low

    wanted = jnp.where(holes_ref[...] >= 0, holes_ref[...] * segments + segment, -1)
    chosen = []
    for pair, first in spans:
        named = sum(load[first + count : first + count + 1, :count] for load in pair).astype(jnp.int32)
        chosen.append(jnp.where(wanted == named, 1.0, 0.0))
    chosen = jnp.concatenate(chosen, axis=1).astype(BF16)
    nn = ((1,), (0,))
    out_ref[...] = dot(chosen, high_ref[...], nn) + dot(chosen, low_ref[...], nn)


def spread(holes, loads, segments, count):
    rows = holes.shape[0]
    height, part = loads[0].shape
    held = (len(loads) + 1) // 2 * (height // (count + 8)) * count
    return pl.pallas_call(
        functools.partial(spread_kernel, count),
        grid=(segments,),
        in_specs=[pl.BlockSpec((rows, 1), lambda i: (0, 0))]
        + [pl.BlockSpec((height, part), lambda i: (0, 0))] * len(loads),
        out_specs=pl.BlockSpec((rows, part), lambda i: (0, i)),
        out_shape=jax.ShapeDtypeStruct((rows, segments * part), F32),
        scratch_shapes=[pltpu.VMEM((held, part), BF16)] * 2,
        compiler_params=pltpu.CompilerParams(vmem_limit_bytes=VMEM_LIMIT),
        cost_estimate=pl.CostEstimate(
            flops=rows * segments * part,
            bytes_accessed=rows * segments * part,
            transcendentals=0,
        ),
        name="spread",
    )(holes, *loads)


def update_kernel(part, core_ref, driving_ref, denominator_ref, kept_ref, received_ref, *refs):
    out_ref = refs[-1]
    for number in range(out_ref.shape[1] // part):
        lanes = slice(number * part, (number + 1) * part)
        half = slice(number // 2 * part, (number // 2 + 1) * part)
        value = jnp.where(core_ref[0] == number % 2, kept_ref[:, half], received_ref[:, half])
        out_ref[:, lanes] = (driving_ref[:, lanes] + value) / denominator_ref[:, lanes]


def update(core, target, driving, denominator, kept, received, offset, part):
    own, width = driving.shape
    size = min(kept.shape[0], own - offset)
    tile = next(rows for rows in (16, 8) if offset % rows == 0 and rows <= size)
    lines = pl.BlockSpec((tile, width), lambda i, core: (offset // tile + i, 0))
    half = pl.BlockSpec((tile, width // 2), lambda i, core: (i, 0))
    return pl.pallas_call(
        functools.partial(update_kernel, part),
        grid_spec=pltpu.PrefetchScalarGridSpec(
            num_scalar_prefetch=1,
            grid=(pl.cdiv(size, tile),),
            in_specs=[lines, lines, half, half] + [pl.BlockSpec(memory_space=pl.ANY)] * len(target),
            out_specs=lines,
        ),
        out_shape=jax.ShapeDtypeStruct((own, width), F32),
        input_output_aliases={5: 0} if target else {},
        compiler_params=pltpu.CompilerParams(vmem_limit_bytes=VMEM_LIMIT),
        cost_estimate=pl.CostEstimate(flops=size * width, bytes_accessed=size * width, transcendentals=0),
        name="update",
    )(core, driving, denominator, kept, received, *target)


def on_device(
    amplitude,
    ladder_coupling,
    crossed_coupling,
    channel_slot,
    channel_of,
    source_row,
    target_row,
    recoupling,
    driving,
    denominator,
):
    groups = lax.axis_size("row")
    columns = lax.axis_size("col")
    depth = columns // 2
    r = lax.axis_index("row")
    c = lax.axis_index("col")
    z, core = c // 2, c % 2
    inner = amplitude.shape[1]
    own = driving.shape[0]
    width = crossed_coupling.shape[1]
    part = width // 2
    count = source_row.shape[1]
    assert depth == groups and amplitude.shape[0] == 2 * own

    across = [[(i, i ^ k) for i in range(groups)] for k in range(1, groups)]
    swap = [(i, i ^ 1) for i in range(columns)]

    def at(array, index):
        return lax.dynamic_index_in_dim(array, index, 0, keepdims=False)

    padded = -(-own // 4) * 4
    sizes = chunk_sizes(padded)
    offsets = [sum(sizes[:k]) for k in range(len(sizes))]
    pairs = jnp.pad(amplitude.reshape(2, own, inner), ((0, 0), (0, padded - own), (0, 0)))
    locals_ = [
        pairs[:, offset : offset + size].reshape(2 * size, inner) for size, offset in zip(sizes, offsets)
    ]

    def spread_first(local, whole):
        return [local] + [lax.ppermute(local, "row", perm) for perm in (across if whole else across[:2])]

    def spread_rest(pieces):
        if len(pieces) == groups:
            return pieces
        cut = pieces[0].shape[0] // 16 * 8
        top = lax.ppermute(pieces[2][:cut], "row", across[0])
        bottom = lax.ppermute(pieces[1][cut:], "row", across[1])
        return [*pieces, top, bottom]

    def tie(*arrays):
        return lax.optimization_barrier(arrays)

    owners = channel_slot[channel_of[0, :, 0]]
    onehot = (owners[:, None] == jnp.arange(groups, dtype=jnp.int32)[None, :]).astype(jnp.int32)
    before = jnp.cumsum(onehot, axis=0) - onehot
    slot = owners * CAP + jnp.sum(before * onehot, axis=1)
    in_slot = slot[None, :] == jnp.arange(groups * CAP, dtype=jnp.int32)[:, None]
    used = jnp.any(in_slot, axis=1)
    source = jnp.sum(jnp.where(in_slot, source_row, 0), axis=1)
    factor = jnp.sum(jnp.where(in_slot, recoupling, 0.0), axis=1)
    per_row = inner // width
    hole, segment = source // per_row, source % per_row
    place = jnp.full_like(hole, -1)
    for size, offset in zip(sizes, offsets):
        inside = hole % own - offset
        spot = 2 * groups * offset + ((hole // (2 * own)) ^ r) * 2 * size + (hole // own % 2) * size + inside
        place = jnp.where((inside >= 0) & (inside < size), spot, place)
    place = jnp.where(used, place, -1)
    names = jnp.pad(target_row[:1].astype(F32), ((0, 7), (0, part - count)))

    last = len(sizes) - 1
    square = groups == 4
    chunks = [spread_rest(spread_first(locals_[0], not square))]
    theirs = jnp.stack([r, 1 - core]).astype(jnp.int32)
    ours = jnp.stack([r, core]).astype(jnp.int32)
    place, segment, factor, names, theirs, ours, *locals_ = tie(
        place[:, None], segment[:, None], factor[:, None], names, theirs, ours, *locals_
    )
    theirs, *chunks[0] = tie(theirs, *chunks[0])

    def gather_chunks():
        held = None
        for kernel in range(last + 1):
            rest = [] if held is None else spread_rest(held)
            first = spread_first(locals_[kernel + 1], not square) if kernel < last else []
            flight = yield None, rest + first
            if rest:
                chunks.append(flight[: len(rest)])
            held = flight[len(rest) :]

    loads = []

    def exchange_segments():
        picked = pick(place, segment, factor, chunks, groups, width)
        arrived = yield picked, [at(picked, r)] + [
            lax.ppermute(at(picked, r ^ k), "row", across[k - 1]) for k in range(1, groups)
        ]
        product = mix(crossed_coupling[0], arrived)
        returned = yield product, [product[0]] + [
            lax.ppermute(product[k], "row", across[k - 1]) for k in range(1, groups)
        ]
        crossed = jnp.concatenate(returned, axis=0)[((slot // CAP) ^ r) * CAP + slot % CAP]
        first = jnp.concatenate([crossed[:, :part], names], axis=0)
        second = jnp.concatenate([crossed[:, part:], names], axis=0)
        to_keep = jnp.where(core == 0, first, second)
        to_send = jnp.where(core == 0, second, first)
        load = jnp.concatenate([to_keep, lax.ppermute(to_send, "col", swap)], axis=0)
        right, left = [load], [load]
        for step in range(depth - 1):
            up = [(i, i + 2) for i in range(columns - 2) if i // 2 >= step]
            down = [(columns - 1 - i, columns - 1 - j) for i, j in up]
            flight = [lax.ppermute(right[-1], "col", up), lax.ppermute(left[-1], "col", down)]
            moved = yield load, flight
            right.append(moved[0])
            left.append(moved[1])
        loads.append(load)
        for k in range(1, depth):
            loads.extend([right[k], left[depth - k]])

    holes = []
    for size, offset in zip(sizes, offsets):
        inside = jnp.tile(jnp.arange(size, dtype=jnp.int32) + offset, 2)
        second = jnp.repeat(jnp.arange(2, dtype=jnp.int32), size)
        holes.append(jnp.where(inside < own, (2 * z + second) * own + inside, -1))
    holes = jnp.concatenate(holes)[:, None]

    lines = [list(range(k, columns, 2)) for k in (0, 1)]
    reduced = {}

    def scatter_line(number, value):
        reduced[number] = lax.psum_scatter(
            value.reshape(depth * 2 * sizes[number], -1),
            "col",
            scatter_dimension=0,
            axis_index_groups=lines,
            tiled=True,
        )

    def walk_line(number, value):
        def own_sum(owner):
            return at(value, jnp.clip(owner, 0, depth - 1))

        right, left = None, None
        for step in range(depth - 1):
            to_right, to_left = own_sum(depth - 1 - step + z), own_sum(z - (depth - 1) + step)
            if step:
                to_right, to_left = to_right + right, to_left + left
            up = [(i, i + 2) for i in range(columns - 2) if i // 2 <= step]
            down = [(columns - 1 - i, columns - 1 - j) for i, j in up]
            right, left = yield None, [lax.ppermute(to_right, "col", up), lax.ppermute(to_left, "col", down)]
        reduced[number] = own_sum(z) + right + left

    gathering, exchanging = gather_chunks(), exchange_segments()
    walks, sent = [], None
    moved = {}

    def begin(stage):
        try:
            return stage.send(moved.pop(stage, None))
        except StopIteration:
            return None, None

    for kernel in range(2 * len(sizes)):
        number, keeping = kernel // 2, kernel % 2
        token, after = (ours, theirs) if keeping else (theirs, ours)
        stages = []
        if kernel < last:
            locals_[kernel + 1], token = tie(locals_[kernel + 1], token)
        if kernel <= last:
            stages.append(gathering)
        else:
            stages.append(exchanging)
        stages += walks
        flights = {}
        for stage in stages:
            ahead, flight = begin(stage)
            if ahead is not None:
                ahead, token = tie(ahead, token)
            if flight is not None:
                flights[stage] = flight
        if keeping:
            received = lax.ppermute(sent, "col", swap)
            value = ladder(token, chunks[number], ladder_coupling, width, received)
        else:
            value = ladder(token, chunks[number], ladder_coupling, width)
        flat = [array for flight in flights.values() for array in flight]
        value, after, *flat = tie(value, after, *flat)
        for stage, flight in flights.items():
            moved[stage], flat = flat[: len(flight)], flat[len(flight) :]
        if kernel == last:
            chunks.append(moved.pop(gathering))
        if not keeping:
            ours, sent = after, value
            continue
        theirs = after
        if number - 1 in reduced:
            value, reduced[number - 1] = tie(value, reduced[number - 1])
        if number < 2:
            scatter_line(number, value)
        else:
            walks.append(walk_line(number, value))
    while len(reduced) < len(sizes) or not loads:
        flights = {stage: begin(stage)[1] for stage in [exchanging] * (not loads) + walks}
        flights = {stage: flight for stage, flight in flights.items() if flight is not None}
        flat = [array for flight in flights.values() for array in flight]
        flat = list(tie(*flat)) if flat else []
        for stage, flight in flights.items():
            moved[stage], flat = flat[: len(flight)], flat[len(flight) :]
    added = spread(holes, loads, ladder_coupling.shape[0] // width, count)

    out = []
    for number, (size, offset) in enumerate(zip(sizes, offsets)):
        line = reduced[number]
        if number == last:
            line, *out = tie(line, *out)
        line = (line + added[2 * offset : 2 * (offset + size)]).reshape(2, size, -1)
        received = lax.ppermute(at(line, 1 - core), "col", swap)
        out = [update(core[None], out, driving, denominator, at(line, core), received, offset, part)]
    return out[0]


def solution(mesh):
    in_specs = (
        P("row", "col"),
        P("row", "col"),
        P("row", None, None),
        P(),
        P("col", "row", None),
        P("col", "row"),
        P("col", "row"),
        P("col", "row"),
        P("col", "row"),
        P("col", "row"),
    )
    out_specs = P("col", "row")
    return jax.shard_map(
        on_device, mesh=mesh, in_specs=in_specs, out_specs=out_specs, check_vma=False
    )
```
